32 devices in a mesh: tm: 4 (over z), chan: 8 (over y, x, core).
Axes of the slice: x: 2, y: 2, z: 4, core: 2. Of those that a mesh axis runs over, the one named last changes fastest.
Arguments:
- voltages: bfloat16 [131072, 2048], P('tm', 'chan'), may hold values from -6 to 6
- band_start: int32 [1], replicated, may hold values from 0 to 992
- feed_map: int32 [2048], replicated, may hold values from 0 to 2047, each once
Outputs:
- visibilities: bfloat16 [32, 2, 2048, 2048], P(('tm', 'chan'))
The draws below stay inside these ranges and needn't reach their ends.
Inputs may be any that keep to these rules, and one draw needn't show every extreme that they name: feed_map names every input once.
All inputs are finite; a program needn't handle non-finite values.
Results may differ from the reference program's by a relative error of at most 0.0079.
Values may be sent and summed in bfloat16 or wider, within the bound.
A program may use at most 128 MiB of HBM per device.

```python
import math
import jax
import jax.numpy as jnp
from jax import lax

INPUTS = 2048
NFFT = 2048
TAPS = 4
SPECTRA = 64
BAND = 32


def shard_levels(rng, dims, shards, least, high):
    loudness = 1.0
    for axis_at, shards_of in shards:
        heights = jax.random.uniform(jax.random.fold_in(jax.random.fold_in(rng, 6), axis_at), (shards_of,), jnp.float32, least / len(shards), high / len(shards))
        loudness = loudness * jnp.repeat(jnp.exp(heights), dims[axis_at] // shards_of).reshape((-1,) + (1,) * (len(dims) - 1 - axis_at))
    return loudness


def noise(rng, dims, scale, reach, split=(), held_as=jnp.bfloat16):
    result = scale * jax.random.normal(rng, dims, jnp.float32)
    if split:
        result = result * shard_levels(rng, dims, split, -0.22, 0.18)
    return jnp.clip(result, -reach, reach).astype(held_as)


def setup_inputs(seed: int = 0) -> dict:
    streams_of = jax.random.split(jax.random.key(seed), 4)
    voltages = noise(streams_of[0], (SPECTRA * NFFT, INPUTS), 1.0, 6.0, ((0, 4), (1, 8)))
    band_start = jax.random.randint(streams_of[1], (1,), 0, NFFT // 2 - BAND + 1).astype(jnp.int32)
    feed_map = jax.random.permutation(streams_of[2], INPUTS).astype(jnp.int32)
    return dict(voltages=voltages, band_start=band_start, feed_map=feed_map)


def taps_window():
    total = TAPS * NFFT
    position = jnp.arange(total, dtype=jnp.float32)
    offset = (position - total / 2 + 0.5) / NFFT
    taper = 0.5 - 0.5 * jnp.cos(2.0 * math.pi * (position + 0.5) / total)
    return (jnp.sinc(offset) * taper).reshape(TAPS, NFFT)

def dft_table(start, count):
    samples = jnp.arange(NFFT, dtype=jnp.int32)
    channel = start + jnp.arange(count, dtype=jnp.int32)
    phase = samples[:, None] * channel[None, :] % NFFT
    angle = 2.0 * math.pi * phase.astype(jnp.float32) / NFFT
    scale = 1.0 / math.sqrt(NFFT)
    return (jnp.concatenate([jnp.cos(angle), -jnp.sin(angle)], 1) * scale).astype(jnp.bfloat16)

def reference(voltages, band_start, feed_map):
    frames = voltages.reshape(SPECTRA, NFFT, INPUTS)
    extended = jnp.concatenate([jnp.zeros((TAPS - 1, NFFT, INPUTS), voltages.dtype), frames], 0)
    window = taps_window()
    table = dft_table(band_start[0], BAND)

    def one_spectrum(index):
        block = lax.dynamic_slice_in_dim(extended, index, TAPS, 0).astype(jnp.float32)
        total = window[0][:, None] * block[0]
        for tap in range(1, TAPS):
            total = total + window[tap][:, None] * block[tap]
        weighted = total.astype(jnp.bfloat16)
        return jnp.dot(weighted.T, table, preferred_element_type=jnp.float32).astype(jnp.bfloat16)
    spectra = lax.map(one_spectrum, jnp.arange(SPECTRA, dtype=jnp.int32))
    grids = spectra.reshape(SPECTRA, INPUTS, 2, BAND).transpose(3, 2, 0, 1)
    ordered = jnp.take(grids, feed_map, axis=3)

    def one_channel(grid):
        real_part = grid[0]
        imag_part = grid[1]
        left_side = jnp.concatenate([real_part, imag_part], 0)
        right_side = jnp.concatenate([imag_part, -real_part], 0)
        cosine_part = jnp.dot(left_side.T, left_side, preferred_element_type=jnp.float32)
        sine_part = jnp.dot(right_side.T, left_side, preferred_element_type=jnp.float32)
        return (jnp.stack([cosine_part, sine_part], 0) / SPECTRA).astype(jnp.bfloat16)
    return lax.map(one_channel, ordered)
```

```python
import functools
import math

import jax
import jax.numpy as jnp
import numpy as np
from jax import lax
from jax.experimental import pallas as pl
from jax.experimental.pallas import tpu as pltpu
from jax.sharding import PartitionSpec as P

NFFT = 2048
TAPS = 4
MESH = pl.DeviceIdType.MESH


def taps_window():
    total = TAPS * NFFT
    position = np.arange(total, dtype=np.float64)
    offset = (position - total / 2 + 0.5) / NFFT
    taper = 0.5 - 0.5 * np.cos(2.0 * math.pi * (position + 0.5) / total)
    return (np.sinc(offset) * taper).reshape(TAPS, NFFT).astype(np.float32)


def base_table(count):
    phase = np.arange(count)[:, None] * np.arange(NFFT)[None, :] % NFFT
    angle = 2.0 * math.pi * phase / NFFT
    scale = 1.0 / math.sqrt(NFFT)
    return np.stack([np.cos(angle) * scale, np.sin(angle) * scale]).astype(np.float32)


def channelize(
    time_count,
    input_count,
    start_ref,
    base_ref,
    window_ref,
    feed_ref,
    volts_ref,
    out_ref,
    volts,
    weights,
    acc,
    carry_out,
    carry_in,
    message,
    received,
    select,
    volts_sem,
    carry_sem,
    send_sem,
    recv_sem,
):
    frames, _, inputs = volts.shape
    count = time_count * input_count
    cols = 2 * count
    half = frames // 2
    tm = lax.axis_index("tm")
    chan = lax.axis_index("chan")
    me = tm * input_count + chan
    keep = TAPS - 1

    def load(frame):
        return pltpu.make_async_copy(
            volts_ref.at[pl.ds(pl.multiple_of(frame * NFFT, NFFT), NFFT), :],
            volts.at[frame],
            volts_sem.at[frame],
        )

    order = list(range(frames - keep, frames)) + list(range(half - keep, frames - keep))
    order += list(range(0, half - keep))
    for frame in order:
        load(frame).start()

    barrier = pltpu.get_barrier_semaphore()

    def greet(step, carry):
        other = lax.rem(me + step, count)
        pl.semaphore_signal(
            barrier,
            inc=1,
            device_id=(other // input_count, lax.rem(other, input_count)),
            device_id_type=MESH,
        )
        return carry

    lax.fori_loop(1, count, greet, 0)

    sample = lax.broadcasted_iota(jnp.int32, (1, NFFT), 1)
    phase = (sample * start_ref[0]) & (NFFT - 1)
    angle = phase.astype(jnp.float32) * (2.0 * math.pi / NFFT)
    turn_cos = jnp.cos(angle)
    turn_sin = jnp.sin(angle)
    base_cos = base_ref[0]
    base_sin = base_ref[1]
    real_rows = base_cos * turn_cos - base_sin * turn_sin
    imag_rows = -(base_sin * turn_cos + base_cos * turn_sin)
    for tap in range(TAPS):
        taper = window_ref[tap : tap + 1, :]
        weights[tap * cols : tap * cols + count, :] = (real_rows * taper).astype(jnp.bfloat16)
        weights[tap * cols + count : (tap + 1) * cols, :] = (imag_rows * taper).astype(jnp.bfloat16)
    acc[...] = jnp.zeros_like(acc)

    def one_frame(frame, carry):
        load(frame).wait()
        result = jnp.dot(weights[...], volts[frame], preferred_element_type=jnp.float32)
        for tap in range(TAPS):
            at = pl.multiple_of((frame + keep - tap) * cols, cols)
            rows = pl.ds(at, cols)
            for lane in range(inputs // 128):
                part = result[tap * cols : (tap + 1) * cols, lane * 128 : (lane + 1) * 128]
                acc[lane, rows, :] = acc[lane, rows, :] + part
        return carry

    lax.fori_loop(frames - keep, frames, one_frame, 0)
    for lane in range(inputs // 128):
        carry_out[:, lane * 128 : (lane + 1) * 128] = acc[lane, frames * cols :, :].astype(
            jnp.bfloat16
        )
    pl.semaphore_wait(barrier, count - 1)

    carry_copy = pltpu.make_async_remote_copy(
        src_ref=carry_out,
        dst_ref=carry_in,
        send_sem=carry_sem.at[0],
        recv_sem=carry_sem.at[1],
        device_id=(lax.rem(tm + 1, time_count), chan),
        device_id_type=MESH,
    )

    @pl.when(tm < time_count - 1)
    def _():
        carry_copy.start()

    def send_half(part):
        def one(step, carry):
            channel = lax.rem(me + step, count)
            first = part * half * cols + channel
            for lane in range(inputs // 128):
                plane = acc.at[lane]
                real = plane[pl.ds(first, half, stride=cols), :]
                imag = plane[pl.ds(first + count, half, stride=cols), :]
                message[part, channel, :, lane * 128 : (lane + 1) * 128] = jnp.concatenate(
                    [real, imag], 0
                ).astype(jnp.bfloat16)

            @pl.when(step < count)
            def _():
                pltpu.make_async_remote_copy(
                    src_ref=message.at[part, channel],
                    dst_ref=received.at[part, chan, tm],
                    send_sem=send_sem.at[part],
                    recv_sem=recv_sem.at[part],
                    device_id=(channel // input_count, lax.rem(channel, input_count)),
                    device_id_type=MESH,
                ).start()

            @pl.when(step == count)
            def _():
                pltpu.make_async_copy(
                    message.at[part, channel], received.at[part, chan, tm], recv_sem.at[part]
                ).start()

            return carry

        lax.fori_loop(1, count + 1, one, 0)

    lax.fori_loop(half - keep, frames - keep, one_frame, 0)
    send_half(1)
    lax.fori_loop(0, half - keep, one_frame, 0)

    @pl.when(tm > 0)
    def _():
        carry_copy.wait_recv()
        for lane in range(inputs // 128):
            before = carry_in[:, lane * 128 : (lane + 1) * 128].astype(jnp.float32)
            acc[lane, : keep * cols, :] = acc[lane, : keep * cols, :] + before

    send_half(0)

    total = input_count * inputs
    block = 256

    def one_select(index, carry):
        at = pl.multiple_of(index * block, block)
        rows = lax.broadcasted_iota(jnp.int32, (block, total), 0) + at
        select[pl.ds(at, block), :] = jnp.where(rows == feed_ref[...], 1.0, 0.0).astype(
            jnp.bfloat16
        )
        return carry

    lax.fori_loop(0, total // block, one_select, 0)

    tall = time_count * 2 * half
    for part in (1, 0):
        pltpu.make_async_copy(received.at[part], received.at[part], recv_sem.at[part]).wait()
        grid = jnp.concatenate(
            [received[part, at].reshape(tall, inputs) for at in range(input_count)], 1
        )

        def one_order(index, carry):
            at = pl.multiple_of(index * block, block)
            out_ref[part * tall : (part + 1) * tall, pl.ds(at, block)] = jnp.dot(
                grid, select[:, pl.ds(at, block)], preferred_element_type=jnp.float32
            ).astype(jnp.bfloat16)
            return carry

        lax.fori_loop(0, total // block, one_order, 0)

    for part in range(2):
        sent = message.at[part, pl.ds(0, count - 1)]
        pltpu.make_async_copy(sent, sent, send_sem.at[part]).wait()

    @pl.when(tm < time_count - 1)
    def _():
        carry_copy.wait_send()


def correlate(half, scale, ordered_ref, out_ref):
    rows = out_ref.shape[2]
    tall = ordered_ref.shape[0]
    at = pl.multiple_of(pl.program_id(0) * rows, rows)
    side = ordered_ref[:, pl.ds(at, rows)].astype(jnp.float32) * scale
    pairs = side.reshape(tall // (2 * half), 2, half, rows)
    turned = jnp.stack([pairs[:, 1], -pairs[:, 0]], 1).reshape(tall, rows)
    for part, left in enumerate((side, turned)):
        out_ref[0, part] = jnp.dot(
            left.T.astype(jnp.bfloat16), ordered_ref[...], preferred_element_type=jnp.float32
        ).astype(jnp.bfloat16)


def on_device(voltages, band_start, feed_map):
    time_count = lax.axis_size("tm")
    input_count = lax.axis_size("chan")
    count = time_count * input_count
    samples, inputs = voltages.shape
    frames = samples // NFFT
    total = input_count * inputs
    cols = 2 * count
    half = frames // 2
    spectra = time_count * frames
    bf16 = jnp.bfloat16
    vmem = pl.BlockSpec(memory_space=pltpu.VMEM)
    keep = TAPS - 1
    ordered = pl.pallas_call(
        functools.partial(channelize, time_count, input_count),
        out_shape=jax.ShapeDtypeStruct((2 * spectra, total), bf16),
        in_specs=[
            pl.BlockSpec(memory_space=pltpu.SMEM),
            vmem,
            vmem,
            vmem,
            pl.BlockSpec(memory_space=pl.ANY),
        ],
        out_specs=vmem,
        scratch_shapes=[
            pltpu.VMEM((frames, NFFT, inputs), bf16),
            pltpu.VMEM((TAPS * cols, NFFT), bf16),
            pltpu.VMEM((inputs // 128, (frames + keep) * cols, 128), jnp.float32),
            pltpu.VMEM((keep * cols, inputs), bf16),
            pltpu.VMEM((keep * cols, inputs), bf16),
            pltpu.VMEM((2, count, 2 * half, inputs), bf16),
            pltpu.VMEM((2, input_count, time_count, 2 * half, inputs), bf16),
            pltpu.VMEM((total, total), bf16),
            pltpu.SemaphoreType.DMA((frames,)),
            pltpu.SemaphoreType.DMA((2,)),
            pltpu.SemaphoreType.DMA((2,)),
            pltpu.SemaphoreType.DMA((2,)),
        ],
        compiler_params=pltpu.CompilerParams(
            collective_id=0, has_side_effects=True, vmem_limit_bytes=50 * 2**20
        ),
        cost_estimate=pl.CostEstimate(
            flops=2 * samples * inputs * TAPS * cols,
            bytes_accessed=samples * inputs * 2,
            transcendentals=0,
        ),
        name="channelize",
    )(
        band_start,
        jnp.asarray(base_table(count)),
        jnp.asarray(taps_window()),
        feed_map.reshape(1, total),
        voltages,
    )
    rows = 256
    return pl.pallas_call(
        functools.partial(correlate, half, 1.0 / spectra),
        grid=(total // rows,),
        out_shape=jax.ShapeDtypeStruct((1, 2, total, total), bf16),
        in_specs=[pl.BlockSpec((2 * spectra, total), lambda i: (0, 0))],
        out_specs=pl.BlockSpec((1, 2, rows, total), lambda i: (0, 0, i, 0)),
        compiler_params=pltpu.CompilerParams(vmem_limit_bytes=50 * 2**20),
        cost_estimate=pl.CostEstimate(
            flops=8 * spectra * total * total,
            bytes_accessed=4 * total * total,
            transcendentals=0,
        ),
        name="correlate",
    )(ordered)


def solution(mesh):
    return jax.shard_map(
        on_device,
        mesh=mesh,
        in_specs=(P("tm", "chan"), P(), P()),
        out_specs=P(("tm", "chan"), None, None, None),
        check_vma=False,
    )
```

```python
import functools
import math

import jax
import jax.numpy as jnp
import numpy as np
from jax import lax
from jax.experimental import pallas as pl
from jax.experimental.pallas import tpu as pltpu
from jax.sharding import PartitionSpec as P

NFFT = 2048
TAPS = 4
MESH = pl.DeviceIdType.MESH


def taps_window():
    total = TAPS * NFFT
    position = np.arange(total, dtype=np.float64)
    offset = (position - total / 2 + 0.5) / NFFT
    taper = 0.5 - 0.5 * np.cos(2.0 * math.pi * (position + 0.5) / total)
    return (np.sinc(offset) * taper).reshape(TAPS, NFFT).astype(np.float32)


def base_table(count):
    phase = np.arange(count)[:, None] * np.arange(NFFT)[None, :] % NFFT
    angle = 2.0 * math.pi * phase / NFFT
    scale = 1.0 / math.sqrt(NFFT)
    return np.stack([np.cos(angle) * scale, np.sin(angle) * scale]).astype(np.float32)


def channelize(
    time_count,
    input_count,
    start_ref,
    base_hbm,
    window_hbm,
    feed_hbm,
    volts_ref,
    out_ref,
    base_ref,
    window_ref,
    feed_ref,
    volts,
    weights,
    acc,
    carry_out,
    carry_in,
    message,
    received,
    select,
    total_acc,
    const_sem,
    volts_sem,
    carry_sem,
    send_sem,
    recv_sem,
):
    frames, _, inputs = volts.shape
    count = time_count * input_count
    cols = 2 * count
    lanes = inputs // 128
    piece = 8 // lanes
    pieces = frames // piece
    tm = lax.axis_index("tm")
    chan = lax.axis_index("chan")
    me = tm * input_count + chan
    keep = TAPS - 1

    def load(frame):
        return pltpu.make_async_copy(
            volts_ref.at[pl.ds(pl.multiple_of(frame * NFFT, NFFT), NFFT), :],
            volts.at[frame],
            volts_sem.at[frame],
        )

    consts = [
        pltpu.make_async_copy(source, target, const_sem.at[index])
        for index, (source, target) in enumerate(
            ((base_hbm, base_ref), (window_hbm, window_ref), (feed_hbm, feed_ref))
        )
    ]
    for copy in consts:
        copy.start()
    for frame in range(frames - keep, frames):
        load(frame).start()

    barrier = pltpu.get_barrier_semaphore()

    def greet(step, carry):
        other = lax.rem(me + step, count)
        pl.semaphore_signal(
            barrier,
            inc=1,
            device_id=(other // input_count, lax.rem(other, input_count)),
            device_id_type=MESH,
        )
        return carry

    lax.fori_loop(1, count, greet, 0)

    sample = lax.broadcasted_iota(jnp.int32, (1, NFFT), 1)
    phase = (sample * start_ref[0]) & (NFFT - 1)
    angle = phase.astype(jnp.float32) * (2.0 * math.pi / NFFT)
    turn_cos = jnp.cos(angle)
    turn_sin = jnp.sin(angle)
    consts[0].wait()
    consts[1].wait()
    for frame in reversed(range(0, frames - keep)):
        load(frame).start()
    base_cos = base_ref[0]
    base_sin = base_ref[1]
    real_rows = base_cos * turn_cos - base_sin * turn_sin
    imag_rows = -(base_sin * turn_cos + base_cos * turn_sin)
    for tap in range(TAPS):
        taper = window_ref[tap : tap + 1, :]
        weights[tap * cols : tap * cols + count, :] = (real_rows * taper).astype(jnp.bfloat16)
        weights[tap * cols + count : (tap + 1) * cols, :] = (imag_rows * taper).astype(jnp.bfloat16)
    acc[...] = jnp.zeros_like(acc)

    total = input_count * inputs
    block = 256

    def some_frames(first, number):
        for index in range(number):
            load(first + index).wait()
        for index in range(number):
            frame = first + index
            result = jnp.dot(weights[...], volts[frame], preferred_element_type=jnp.float32)
            for tap in range(TAPS):
                rows = pl.ds(pl.multiple_of((frame + keep - tap) * cols, cols), cols)
                for lane in range(lanes):
                    part = result[tap * cols : (tap + 1) * cols, lane * 128 : (lane + 1) * 128]
                    acc[lane, rows, :] = acc[lane, rows, :] + part

    some_frames(frames - keep, keep)
    for lane in range(inputs // 128):
        carry_out[:, lane * 128 : (lane + 1) * 128] = acc[lane, frames * cols :, :].astype(
            jnp.bfloat16
        )
    pl.semaphore_wait(barrier, count - 1)

    carry_copy = pltpu.make_async_remote_copy(
        src_ref=carry_out,
        dst_ref=carry_in,
        send_sem=carry_sem.at[0],
        recv_sem=carry_sem.at[1],
        device_id=(lax.rem(tm + 1, time_count), chan),
        device_id_type=MESH,
    )

    @pl.when(tm < time_count - 1)
    def _():
        carry_copy.start()

    def send_piece(index):
        def one(step, carry):
            to_chan = lax.rem(chan + step // time_count, input_count)
            to_time = lax.rem(tm + 1 + lax.rem(step, time_count), time_count)
            channel = to_time * input_count + to_chan
            first = index * piece * cols + channel
            rows = [acc.at[lane][pl.ds(first, 2 * piece, stride=count), :] for lane in range(lanes)]
            message[channel, index] = jnp.concatenate(rows, 0).astype(jnp.bfloat16)

            @pl.when(channel != me)
            def _():
                pltpu.make_async_remote_copy(
                    src_ref=message.at[channel, index],
                    dst_ref=received.at[chan, index, tm],
                    send_sem=send_sem,
                    recv_sem=recv_sem.at[chan],
                    device_id=(to_time, to_chan),
                    device_id_type=MESH,
                ).start()

            @pl.when(channel == me)
            def _():
                pltpu.make_async_copy(
                    message.at[channel, index], received.at[chan, index, tm], recv_sem.at[chan]
                ).start()

            return carry

        lax.fori_loop(0, count, one, 0)

    def one_piece(step, carry):
        index = pieces - 1 - step
        some_frames(index * piece - keep, piece)
        send_piece(index)
        return carry

    lax.fori_loop(0, pieces - 1, one_piece, 0)
    some_frames(0, piece - keep)

    @pl.when(tm > 0)
    def _():
        carry_copy.wait_recv()
        for lane in range(lanes):
            before = carry_in[:, lane * 128 : (lane + 1) * 128].astype(jnp.float32)
            acc[lane, : keep * cols, :] = acc[lane, : keep * cols, :] + before

    send_piece(0)

    consts[2].wait()

    def one_select(index, carry):
        at = pl.multiple_of(index * block, block)
        rows = lax.broadcasted_iota(jnp.int32, (block, total), 0) + at
        select[pl.ds(at, block), :] = jnp.where(rows == feed_ref[...], 1.0, 0.0).astype(
            jnp.bfloat16
        )
        return carry

    lax.fori_loop(0, total // block, one_select, 0)

    tall = time_count * 2 * frames
    total_acc[...] = jnp.zeros_like(total_acc)
    wide = 512

    def one_source(step, carry):
        source = lax.rem(chan - step + input_count, input_count)
        landed = received.at[source]
        pltpu.make_async_copy(landed, landed, recv_sem.at[source]).wait()
        grid = received[source].astype(jnp.float32)
        grid = grid.reshape(pieces * time_count, lanes, 2 * piece, 128)
        grid = jnp.concatenate([grid[:, lane] for lane in range(lanes)], 2)
        grid = grid.reshape(tall, inputs).astype(jnp.bfloat16)
        own_rows = pl.ds(pl.multiple_of(source * inputs, inputs), inputs)

        def one_order(index, carry):
            at = pl.ds(pl.multiple_of(index * wide, wide), wide)
            total_acc[:, at] = total_acc[:, at] + jnp.dot(
                grid, select[own_rows, at], preferred_element_type=jnp.float32
            )
            return carry

        lax.fori_loop(0, total // wide, one_order, 0)
        return carry

    lax.fori_loop(0, input_count, one_source, 0)
    out_ref[...] = total_acc[...].astype(jnp.bfloat16)

    sent = message.at[pl.ds(0, count - 1)]
    pltpu.make_async_copy(sent, sent, send_sem).wait()

    @pl.when(tm < time_count - 1)
    def _():
        carry_copy.wait_send()


def correlate(scale, ordered_ref, out_ref):
    rows, total = out_ref.shape[2:]
    tall = ordered_ref.shape[0]
    at = pl.multiple_of(pl.program_id(0) * rows, rows)
    side = ordered_ref[:, pl.ds(at, rows)].astype(jnp.float32) * scale
    row = lax.broadcasted_iota(jnp.int32, (tall, rows), 0)
    turned = jnp.where(
        (row & 1) == 0, pltpu.roll(side, tall - 1, 0), -pltpu.roll(side, 1, 0)
    )
    left = jnp.concatenate([side, turned], 1).astype(jnp.bfloat16)
    both = lax.dot_general(
        left, ordered_ref[...], (((0,), (0,)), ((), ())), preferred_element_type=jnp.float32
    )
    out_ref[0] = both.astype(jnp.bfloat16).reshape(2, rows, total)


def on_device(voltages, band_start, feed_map):
    time_count = lax.axis_size("tm")
    input_count = lax.axis_size("chan")
    count = time_count * input_count
    samples, inputs = voltages.shape
    frames = samples // NFFT
    total = input_count * inputs
    cols = 2 * count
    pieces = frames * inputs // 1024
    spectra = time_count * frames
    bf16 = jnp.bfloat16
    vmem = pl.BlockSpec(memory_space=pltpu.VMEM)
    keep = TAPS - 1
    ordered = pl.pallas_call(
        functools.partial(channelize, time_count, input_count),
        out_shape=jax.ShapeDtypeStruct((2 * spectra, total), bf16),
        in_specs=[pl.BlockSpec(memory_space=pltpu.SMEM)] + [pl.BlockSpec(memory_space=pl.ANY)] * 4,
        out_specs=vmem,
        scratch_shapes=[
            pltpu.VMEM((2, count, NFFT), jnp.float32),
            pltpu.VMEM((TAPS, NFFT), jnp.float32),
            pltpu.VMEM((1, total), jnp.int32),
            pltpu.VMEM((frames, NFFT, inputs), bf16),
            pltpu.VMEM((TAPS * cols, NFFT), bf16),
            pltpu.VMEM((inputs // 128, (frames + keep) * cols, 128), jnp.float32),
            pltpu.VMEM((keep * cols, inputs), bf16),
            pltpu.VMEM((keep * cols, inputs), bf16),
            pltpu.VMEM((count, pieces, 16, 128), bf16),
            pltpu.VMEM((input_count, pieces, time_count, 16, 128), bf16),
            pltpu.VMEM((total, total), bf16),
            pltpu.VMEM((2 * spectra, total), jnp.float32),
            pltpu.SemaphoreType.DMA((3,)),
            pltpu.SemaphoreType.DMA((frames,)),
            pltpu.SemaphoreType.DMA((2,)),
            pltpu.SemaphoreType.DMA,
            pltpu.SemaphoreType.DMA((input_count,)),
        ],
        compiler_params=pltpu.CompilerParams(
            collective_id=0, has_side_effects=True, vmem_limit_bytes=60 * 2**20
        ),
        cost_estimate=pl.CostEstimate(
            flops=2 * samples * inputs * TAPS * cols,
            bytes_accessed=samples * inputs * 2,
            transcendentals=0,
        ),
        name="channelize",
    )(
        band_start,
        jnp.asarray(base_table(count)),
        jnp.asarray(taps_window()),
        feed_map.reshape(1, total),
        voltages,
    )
    rows = 512
    return pl.pallas_call(
        functools.partial(correlate, 1.0 / spectra),
        grid=(total // rows,),
        out_shape=jax.ShapeDtypeStruct((1, 2, total, total), bf16),
        in_specs=[pl.BlockSpec((2 * spectra, total), lambda i: (0, 0))],
        out_specs=pl.BlockSpec((1, 2, rows, total), lambda i: (0, 0, i, 0)),
        compiler_params=pltpu.CompilerParams(vmem_limit_bytes=60 * 2**20),
        cost_estimate=pl.CostEstimate(
            flops=8 * spectra * total * total,
            bytes_accessed=4 * total * total,
            transcendentals=0,
        ),
        name="correlate",
    )(ordered)


def solution(mesh):
    return jax.shard_map(
        on_device,
        mesh=mesh,
        in_specs=(P("tm", "chan"), P(), P()),
        out_specs=P(("tm", "chan"), None, None, None),
        check_vma=False,
    )
```

```python
import functools
import math

import jax
import jax.numpy as jnp
import numpy as np
from jax import lax
from jax.experimental import pallas as pl
from jax.experimental.pallas import tpu as pltpu
from jax.sharding import PartitionSpec as P

NFFT = 2048
TAPS = 4
MESH = pl.DeviceIdType.MESH


def taps_window():
    total = TAPS * NFFT
    position = np.arange(total, dtype=np.float64)
    offset = (position - total / 2 + 0.5) / NFFT
    taper = 0.5 - 0.5 * np.cos(2.0 * math.pi * (position + 0.5) / total)
    return (np.sinc(offset) * taper).reshape(TAPS, NFFT).astype(np.float32)


def base_table(count):
    phase = np.arange(count)[:, None] * np.arange(NFFT)[None, :] % NFFT
    angle = 2.0 * math.pi * phase / NFFT
    scale = 1.0 / math.sqrt(NFFT)
    return np.stack([np.cos(angle) * scale, np.sin(angle) * scale]).astype(np.float32)


def channelize(
    time_count,
    input_count,
    start_ref,
    base_hbm,
    window_hbm,
    feed_hbm,
    volts_ref,
    out_ref,
    base_ref,
    window_ref,
    feed_ref,
    volts,
    weights,
    acc,
    carry_out,
    carry_in,
    message,
    received,
    select,
    const_sem,
    volts_sem,
    carry_sem,
    send_sem,
    recv_sem,
):
    frames, _, inputs = volts.shape
    count = time_count * input_count
    cols = 2 * count
    half = frames // 2
    tm = lax.axis_index("tm")
    chan = lax.axis_index("chan")
    me = tm * input_count + chan
    keep = TAPS - 1

    def load(frame):
        return pltpu.make_async_copy(
            volts_ref.at[pl.ds(pl.multiple_of(frame * NFFT, NFFT), NFFT), :],
            volts.at[frame],
            volts_sem.at[frame],
        )

    consts = [
        pltpu.make_async_copy(source, target, const_sem.at[index])
        for index, (source, target) in enumerate(
            ((base_hbm, base_ref), (window_hbm, window_ref), (feed_hbm, feed_ref))
        )
    ]
    for copy in consts:
        copy.start()
    order = list(range(frames - keep, frames)) + list(range(half - keep, frames - keep))
    order += list(range(0, half - keep))
    for frame in order:
        load(frame).start()

    barrier = pltpu.get_barrier_semaphore()

    def greet(step, carry):
        other = lax.rem(me + step, count)
        pl.semaphore_signal(
            barrier,
            inc=1,
            device_id=(other // input_count, lax.rem(other, input_count)),
            device_id_type=MESH,
        )
        return carry

    lax.fori_loop(1, count, greet, 0)

    sample = lax.broadcasted_iota(jnp.int32, (1, NFFT), 1)
    phase = (sample * start_ref[0]) & (NFFT - 1)
    angle = phase.astype(jnp.float32) * (2.0 * math.pi / NFFT)
    turn_cos = jnp.cos(angle)
    turn_sin = jnp.sin(angle)
    consts[0].wait()
    consts[1].wait()
    base_cos = base_ref[0]
    base_sin = base_ref[1]
    real_rows = base_cos * turn_cos - base_sin * turn_sin
    imag_rows = -(base_sin * turn_cos + base_cos * turn_sin)
    for tap in range(TAPS):
        taper = window_ref[tap : tap + 1, :]
        weights[tap * cols : tap * cols + count, :] = (real_rows * taper).astype(jnp.bfloat16)
        weights[tap * cols + count : (tap + 1) * cols, :] = (imag_rows * taper).astype(jnp.bfloat16)
    acc[...] = jnp.zeros_like(acc)

    total = input_count * inputs
    block = 256
    lanes = inputs // 128

    def some_frames(first, number):
        for index in range(number):
            load(first + index).wait()
        for index in range(number):
            frame = first + index
            result = jnp.dot(weights[...], volts[frame], preferred_element_type=jnp.float32)
            for tap in range(TAPS):
                rows = pl.ds(pl.multiple_of((frame + keep - tap) * cols, cols), cols)
                for lane in range(lanes):
                    part = result[tap * cols : (tap + 1) * cols, lane * 128 : (lane + 1) * 128]
                    acc[lane, rows, :] = acc[lane, rows, :] + part

    some_frames(frames - keep, keep)
    for lane in range(inputs // 128):
        carry_out[:, lane * 128 : (lane + 1) * 128] = acc[lane, frames * cols :, :].astype(
            jnp.bfloat16
        )
    pl.semaphore_wait(barrier, count - 1)

    carry_copy = pltpu.make_async_remote_copy(
        src_ref=carry_out,
        dst_ref=carry_in,
        send_sem=carry_sem.at[0],
        recv_sem=carry_sem.at[1],
        device_id=(lax.rem(tm + 1, time_count), chan),
        device_id_type=MESH,
    )

    @pl.when(tm < time_count - 1)
    def _():
        carry_copy.start()

    def send_half(part):
        def one(step, carry):
            channel = lax.rem(me + step, count)
            first = part * half * cols + channel
            for lane in range(inputs // 128):
                plane = acc.at[lane]
                real = plane[pl.ds(first, half, stride=cols), :]
                imag = plane[pl.ds(first + count, half, stride=cols), :]
                message[part, channel, :, lane * 128 : (lane + 1) * 128] = jnp.concatenate(
                    [real, imag], 0
                ).astype(jnp.bfloat16)

            @pl.when(step < count)
            def _():
                pltpu.make_async_remote_copy(
                    src_ref=message.at[part, channel],
                    dst_ref=received.at[part, chan, tm],
                    send_sem=send_sem.at[part],
                    recv_sem=recv_sem.at[part],
                    device_id=(channel // input_count, lax.rem(channel, input_count)),
                    device_id_type=MESH,
                ).start()

            @pl.when(step == count)
            def _():
                pltpu.make_async_copy(
                    message.at[part, channel], received.at[part, chan, tm], recv_sem.at[part]
                ).start()

            return carry

        lax.fori_loop(1, count + 1, one, 0)

    group = half // 2

    def one_group(index, carry):
        some_frames(half - keep + index * group, group)
        return carry

    lax.fori_loop(0, half // group, one_group, 0)
    send_half(1)
    some_frames(0, half - keep)

    @pl.when(tm > 0)
    def _():
        carry_copy.wait_recv()
        for lane in range(inputs // 128):
            before = carry_in[:, lane * 128 : (lane + 1) * 128].astype(jnp.float32)
            acc[lane, : keep * cols, :] = acc[lane, : keep * cols, :] + before

    send_half(0)

    consts[2].wait()

    def one_select(index, carry):
        at = pl.multiple_of(index * block, block)
        rows = lax.broadcasted_iota(jnp.int32, (block, total), 0) + at
        select[pl.ds(at, block), :] = jnp.where(rows == feed_ref[...], 1.0, 0.0).astype(
            jnp.bfloat16
        )
        return carry

    lax.fori_loop(0, total // block, one_select, 0)

    tall = time_count * 2 * half
    for part in (1, 0):
        pltpu.make_async_copy(received.at[part], received.at[part], recv_sem.at[part]).wait()
        grid = jnp.concatenate(
            [received[part, at].reshape(tall, inputs) for at in range(input_count)], 1
        )

        def one_order(index, carry):
            at = pl.multiple_of(index * block, block)
            rows = slice(part * tall, (part + 1) * tall)
            side = jnp.dot(
                grid, select[:, pl.ds(at, block)], preferred_element_type=jnp.float32
            )
            out_ref[rows, pl.ds(at, block)] = side.astype(jnp.bfloat16)
            return carry

        lax.fori_loop(0, total // block, one_order, 0)

    for part in range(2):
        sent = message.at[part, pl.ds(0, count - 1)]
        pltpu.make_async_copy(sent, sent, send_sem.at[part]).wait()

    @pl.when(tm < time_count - 1)
    def _():
        carry_copy.wait_send()


def correlate(half, scale, ordered_ref, out_ref):
    rows, total = out_ref.shape[2:]
    tall = ordered_ref.shape[0]
    at = pl.multiple_of(pl.program_id(0) * rows, rows)
    side = ordered_ref[:, pl.ds(at, rows)].astype(jnp.float32) * scale
    pairs = side.reshape(tall // (2 * half), 2, half, rows)
    turned = jnp.stack([pairs[:, 1], -pairs[:, 0]], 1).reshape(tall, rows)
    left = jnp.concatenate([side, turned], 1).astype(jnp.bfloat16)
    both = lax.dot_general(
        left, ordered_ref[...], (((0,), (0,)), ((), ())), preferred_element_type=jnp.float32
    )
    out_ref[0] = both.astype(jnp.bfloat16).reshape(2, rows, total)


def on_device(voltages, band_start, feed_map):
    time_count = lax.axis_size("tm")
    input_count = lax.axis_size("chan")
    count = time_count * input_count
    samples, inputs = voltages.shape
    frames = samples // NFFT
    total = input_count * inputs
    cols = 2 * count
    half = frames // 2
    spectra = time_count * frames
    bf16 = jnp.bfloat16
    vmem = pl.BlockSpec(memory_space=pltpu.VMEM)
    keep = TAPS - 1
    ordered = pl.pallas_call(
        functools.partial(channelize, time_count, input_count),
        out_shape=jax.ShapeDtypeStruct((2 * spectra, total), bf16),
        in_specs=[pl.BlockSpec(memory_space=pltpu.SMEM)] + [pl.BlockSpec(memory_space=pl.ANY)] * 4,
        out_specs=vmem,
        scratch_shapes=[
            pltpu.VMEM((2, count, NFFT), jnp.float32),
            pltpu.VMEM((TAPS, NFFT), jnp.float32),
            pltpu.VMEM((1, total), jnp.int32),
            pltpu.VMEM((frames, NFFT, inputs), bf16),
            pltpu.VMEM((TAPS * cols, NFFT), bf16),
            pltpu.VMEM((inputs // 128, (frames + keep) * cols, 128), jnp.float32),
            pltpu.VMEM((keep * cols, inputs), bf16),
            pltpu.VMEM((keep * cols, inputs), bf16),
            pltpu.VMEM((2, count, 2 * half, inputs), bf16),
            pltpu.VMEM((2, input_count, time_count, 2 * half, inputs), bf16),
            pltpu.VMEM((total, total), bf16),
            pltpu.SemaphoreType.DMA((3,)),
            pltpu.SemaphoreType.DMA((frames,)),
            pltpu.SemaphoreType.DMA((2,)),
            pltpu.SemaphoreType.DMA((2,)),
            pltpu.SemaphoreType.DMA((2,)),
        ],
        compiler_params=pltpu.CompilerParams(
            collective_id=0, has_side_effects=True, vmem_limit_bytes=50 * 2**20
        ),
        cost_estimate=pl.CostEstimate(
            flops=2 * samples * inputs * TAPS * cols,
            bytes_accessed=samples * inputs * 2,
            transcendentals=0,
        ),
        name="channelize",
    )(
        band_start,
        jnp.asarray(base_table(count)),
        jnp.asarray(taps_window()),
        feed_map.reshape(1, total),
        voltages,
    )
    rows = 512
    return pl.pallas_call(
        functools.partial(correlate, half, 1.0 / spectra),
        grid=(total // rows,),
        out_shape=jax.ShapeDtypeStruct((1, 2, total, total), bf16),
        in_specs=[pl.BlockSpec((2 * spectra, total), lambda i: (0, 0))],
        out_specs=pl.BlockSpec((1, 2, rows, total), lambda i: (0, 0, i, 0)),
        compiler_params=pltpu.CompilerParams(vmem_limit_bytes=50 * 2**20),
        cost_estimate=pl.CostEstimate(
            flops=8 * spectra * total * total,
            bytes_accessed=4 * total * total,
            transcendentals=0,
        ),
        name="correlate",
    )(ordered)


def solution(mesh):
    return jax.shard_map(
        on_device,
        mesh=mesh,
        in_specs=(P("tm", "chan"), P(), P()),
        out_specs=P(("tm", "chan"), None, None, None),
        check_vma=False,
    )
```
